32 devices in a mesh: parts: 2 (over y), elem: 4 (over x, core), dir: 4 (over z).
Axes of the slice: x: 2, y: 2, z: 4, core: 2. Of those that a mesh axis runs over, the one named last changes fastest.
Arguments:
- surface: bfloat16 [32768, 128], P(('parts', 'elem', 'dir')), parts along dimension 0, may hold values from -5 to 5
- centres: float32 [3, 16384], P(None, ('elem', 'dir')), may hold values from -4 to 4
- patch_of: int32 [16384], P(('elem', 'dir')), may hold values from 0 to 63
- panels: float32 [4, 64], P(None, 'elem'), may hold values from -1 to 2, as said below
- dir_index: int32 [4096], replicated, may hold values from 0 to 16379
- wavenumber: float32 [2], P('parts'), parts along dimension 0, may hold values from 4 to 12
Outputs:
- far_field: float32 [4, 32, 4096], P('parts', None, ('elem', 'dir')), parts along dimension 0
The draws below stay inside these ranges and needn't reach their ends.
There are 2 independent parts, one for each index of `parts`. The reference program is written for one: setup_inputs(seed, part) draws one part's arguments, and reference() takes and returns one part's arrays. A program takes and returns all parts, laid end to end along the dimension named above; an argument that names none is the same for every part. Nothing has to cross between parts.
Inputs may be any that keep to these rules, and one draw needn't show every extreme that they name: `panels`: rows 0 to 2 of each column form a unit vector; row 3 is positive.
All inputs are finite; a program needn't handle non-finite values.
Results may differ from the reference program's by a relative error of at most 0.0029.
Values may be sent and summed in bfloat16 or wider, within the bound.
A program may use at most 64 MiB of HBM per device.

```python
import math
import jax
import jax.numpy as jnp
from jax import lax

CASES = 32
BOXES = 16
DIRS = 4096
GRID_THETA = 91
GRID_PHI = 180
PATCHES = 64
ELEMENTS = 16384


def draw_surface(key, part):
    key = jax.random.fold_in(key, 5)
    first_key = jax.random.fold_in(key, 0)
    row_index = jnp.arange(ELEMENTS, dtype=jnp.int32)
    box_index = row_index * BOXES // ELEMENTS
    case_index = jnp.arange(4 * CASES, dtype=jnp.int32) % CASES
    loudness = jnp.where(box_index[:, None] == case_index[None, :] // 2, 1.0, 0.25)
    values = jax.random.normal(first_key, (ELEMENTS, 4 * CASES), jnp.float32)
    return jnp.clip(values * loudness, -5.0, 5.0).astype(jnp.bfloat16)


def draw_centres(key, part):
    key = jax.random.fold_in(key, 3)
    first_key, second_key, third_key = jax.random.split(key, 3)
    box_index = (jnp.arange(ELEMENTS, dtype=jnp.int32) * BOXES // ELEMENTS).astype(jnp.float32)
    across = jax.random.uniform(first_key, (ELEMENTS,), jnp.float32, -4.0, 4.0)
    depth_pos = jax.random.uniform(second_key, (ELEMENTS,), jnp.float32, -4.0, 4.0)
    height = (box_index - BOXES / 2.0) * 0.45 + jax.random.uniform(third_key, (ELEMENTS,), jnp.float32, 0.0, 0.4)
    return jnp.stack([across, depth_pos, height]).astype(jnp.float32)


def draw_panels(key, part):
    key = jax.random.fold_in(key, 7)
    first_key, second_key, third_key = jax.random.split(key, 3)
    polar_angle = jax.random.uniform(first_key, (PATCHES,), jnp.float32, 0.0, math.pi)
    azimuth = jax.random.uniform(second_key, (PATCHES,), jnp.float32, -math.pi, math.pi)
    panel_area = jnp.exp(jax.random.uniform(third_key, (PATCHES,), jnp.float32, math.log(0.5), math.log(2.0)))
    return jnp.stack([jnp.sin(polar_angle) * jnp.cos(azimuth), jnp.sin(polar_angle) * jnp.sin(azimuth), jnp.cos(polar_angle), panel_area]).astype(jnp.float32)


def with_ends(array, key, least, top_value):
    longest = array.shape.index(max(array.shape))
    spots = []
    for shift in (0, 1):
        where = [jax.random.randint(jax.random.fold_in(key, axis), (), 0, length) for axis, length in enumerate(array.shape)]
        where[longest] = (where[longest] + shift) % array.shape[longest]
        spots.append(tuple(where))
    return array.at[spots[0]].set(least).at[spots[1]].set(top_value)


def setup_inputs(seed: int = 0, part: int = 0) -> dict:
    seeds = jax.random.split(jax.random.key(seed), 7)
    part_keys = jax.random.split(jax.random.fold_in(seeds[6], part), 7)
    surface = draw_surface(jax.random.fold_in(jax.random.fold_in(seeds[6], part), 71), part)
    centres = draw_centres(jax.random.fold_in(seeds[6], 71), part)
    patch_of = with_ends(jax.random.randint(seeds[2], (ELEMENTS,), 0, PATCHES), jax.random.fold_in(seeds[2], 1), 0, PATCHES - 1).astype(jnp.int32)
    panels = draw_panels(jax.random.fold_in(seeds[6], 71), part)
    dir_index = with_ends(jax.random.randint(seeds[4], (DIRS,), 0, GRID_THETA * GRID_PHI), jax.random.fold_in(seeds[4], 1), 0, (GRID_THETA * GRID_PHI) - 1).astype(jnp.int32)
    wavenumber = jnp.clip(jax.random.uniform(part_keys[5], (1,), jnp.float32, 4.0, 12.0), 4.0, 12.0)
    return {"surface": surface, "centres": centres, "patch_of": patch_of, "panels": panels, "dir_index": dir_index, "wavenumber": wavenumber}


def unit_vectors(dir_index):
    polar_index = dir_index // GRID_PHI
    azimuth_index = dir_index % GRID_PHI
    polar_angle = polar_index.astype(jnp.float32) * (math.pi / (GRID_THETA - 1))
    azimuth = azimuth_index.astype(jnp.float32) * (2.0 * math.pi / GRID_PHI)
    return jnp.stack([jnp.sin(polar_angle) * jnp.cos(azimuth), jnp.sin(polar_angle) * jnp.sin(azimuth), jnp.cos(polar_angle)])

def far_block(fields, places, facets, unit_dirs, wave_number):
    phase_angle = wave_number * (places[0][:, None] * unit_dirs[0][None, :] + places[1][:, None] * unit_dirs[1][None, :] + places[2][:, None] * unit_dirs[2][None, :])
    facing = facets[0][:, None] * unit_dirs[0][None, :] + facets[1][:, None] * unit_dirs[1][None, :] + facets[2][:, None] * unit_dirs[2][None, :]
    mono_real = facets[3][:, None] * jnp.cos(phase_angle)
    mono_imag = -facets[3][:, None] * jnp.sin(phase_angle)
    dipole = jnp.concatenate([mono_real * facing, mono_imag * facing], axis=1).astype(jnp.bfloat16)
    monopole = jnp.concatenate([mono_real, mono_imag], axis=1).astype(jnp.bfloat16)
    contract = (((0,), (0,)), ((), ()))
    half_width = fields.shape[1] // 2
    dipole_part = lax.dot_general(fields[:, :half_width], dipole, contract, preferred_element_type=jnp.float32)
    monopole_part = lax.dot_general(fields[:, half_width:], monopole, contract, preferred_element_type=jnp.float32)
    case_count = half_width // 2
    block_width = unit_dirs.shape[1]
    sum_real = dipole_part[:case_count, :block_width] - dipole_part[case_count:, block_width:] + monopole_part[:case_count, :block_width] - monopole_part[case_count:, block_width:]
    sum_imag = dipole_part[case_count:, :block_width] + dipole_part[:case_count, block_width:] + monopole_part[case_count:, :block_width] + monopole_part[:case_count, block_width:]
    return jnp.stack([sum_real, sum_imag])

def reference(surface, centres, patch_of, panels, dir_index, wavenumber):
    wave_number = wavenumber[0]
    facets = panels[:, patch_of]
    unit_dirs = unit_vectors(dir_index)
    block_width = min(512, DIRS)
    block_count = DIRS // block_width
    dir_blocks = unit_dirs.reshape(3, block_count, block_width).transpose(1, 0, 2)
    block_rows = math.gcd(ELEMENTS, 8192)
    row_blocks = ELEMENTS // block_rows

    def one_block(direction_block):

        def add_rows(running, block_index):
            first_row = (block_index * block_rows).astype(jnp.int32)
            fields = lax.dynamic_slice_in_dim(surface, first_row, block_rows, 0)
            places = lax.dynamic_slice_in_dim(centres, first_row, block_rows, 1)
            facet_rows = lax.dynamic_slice_in_dim(facets, first_row, block_rows, 1)
            return (running + far_block(fields, places, facet_rows, direction_block, wave_number), None)
        zeros_init = jnp.zeros((2, CASES, block_width), jnp.float32)
        running, unused = lax.scan(add_rows, zeros_init, jnp.arange(row_blocks, dtype=jnp.int32))
        return running
    partials = lax.map(one_block, dir_blocks)
    summed = partials.transpose(1, 2, 0, 3).reshape(2, CASES, DIRS)
    far_scale = wave_number / (4.0 * math.pi * math.sqrt(ELEMENTS))
    return jnp.stack([far_scale * summed[1], -far_scale * summed[0]])
```

```python
import functools
import math

import jax
import jax.numpy as jnp
import numpy as np
from jax import lax
from jax.experimental import pallas as pl
from jax.experimental.pallas import tpu as pltpu
from jax.sharding import PartitionSpec as P

GRID_THETA = 91
GRID_PHI = 180
QUARTER = GRID_PHI // 4
SPLIT_ROWS = 32
TILE = 256
MESH = pl.DeviceIdType.MESH


def fit_even(function, degree, top):
    nodes = np.cos((np.arange(400) + 0.5) * np.pi / 800)
    scaled = nodes * top
    basis = np.stack([scaled ** (2 * power) for power in range(degree + 1)], axis=1)
    weights, *_ = np.linalg.lstsq(basis / 1.0, function(scaled), rcond=None)
    return [float(weight) for weight in weights]


SIN_TURN = fit_even(lambda r: np.sin(2 * np.pi * r) / r, 5, 0.5)
COS_TURN = fit_even(lambda r: np.cos(2 * np.pi * r), 5, 0.5)
SIN_QUARTER = fit_even(lambda r: np.sin(2 * np.pi * r) / r, 6, 0.25)


def horner(weights, z):
    value = jnp.float32(weights[-1])
    for weight in weights[-2::-1]:
        value = value * z + jnp.float32(weight)
    return value


def splits(value):
    high = value.astype(jnp.bfloat16).astype(jnp.float32)
    rest = value - high
    middle = rest.astype(jnp.bfloat16).astype(jnp.float32)
    low = (rest - middle).astype(jnp.bfloat16).astype(jnp.float32)
    return high, middle, low


def grid_directions(dir_row):
    polar = jnp.floor((dir_row.astype(jnp.float32) + 0.5) * (1.0 / GRID_PHI))
    azimuth = dir_row.astype(jnp.float32) - polar * GRID_PHI
    row = lax.broadcasted_iota(jnp.int32, (8, dir_row.shape[1]), 0)
    steps = jnp.where(row < 2, polar, azimuth)
    steps = steps + jnp.where(row % 2 == 1, float(QUARTER), 0.0)
    steps = jnp.where(steps >= 2.0 * QUARTER, steps - 4.0 * QUARTER, steps)
    steps = jnp.where(steps > QUARTER, 2.0 * QUARTER - steps, steps)
    steps = jnp.where(steps < -QUARTER, -2.0 * QUARTER - steps, steps)
    turns = steps * (1.0 / GRID_PHI)
    sines = turns * horner(SIN_QUARTER, turns * turns)
    return sines[0:1] * sines[3:4], sines[0:1] * sines[2:3], sines[1:2]


def kernel(
    n_elem, n_dir,
    wave_ref, surface_ref, centres_ref, patch_ref, panels_ref, dir_ref, out_ref,
    panel_slots, unit_rows, unit_split, place_split, area_cols, weights, outbox, inbox, total,
    panel_send, panel_recv, send_sem, recv_sem,
):
    my_elem, my_dir = lax.axis_index("elem"), lax.axis_index("dir")
    me = my_elem * n_dir + my_dir
    group = n_elem * n_dir
    elements = surface_ref.shape[0]
    width = out_ref.shape[1]
    half = surface_ref.shape[1] // 2
    cases = half // 2
    panel_count = panels_ref.shape[1]

    barrier = pltpu.get_barrier_semaphore()

    def greet(step, carry):
        other = lax.rem(me + step, group)
        pl.semaphore_signal(
            barrier, inc=1,
            device_id={"elem": other // n_dir, "dir": lax.rem(other, n_dir)},
            device_id_type=MESH,
        )
        return carry

    lax.fori_loop(1, group, greet, 0)

    panel_slots[my_elem] = jnp.zeros((8, 128), jnp.float32)
    panel_slots[my_elem, 0:4, 0:panel_count] = panels_ref[...]

    ux, uy, uz = grid_directions(dir_ref[...])
    unit_rows[0:1, :] = ux
    unit_rows[1:2, :] = uy
    unit_rows[2:3, :] = uz
    uh, um, ul = zip(*[splits(u) for u in (ux, uy, uz)])
    pad = jnp.zeros((SPLIT_ROWS - 18, ux.shape[1]), jnp.float32)
    unit_split[...] = jnp.concatenate(
        [*uh, *um, *uh, *um, *ul, *uh, pad], axis=0
    ).astype(jnp.bfloat16)

    wave = wave_ref[0]
    places = centres_ref[...] * (wave * (0.5 / math.pi))
    ch, cm, cl = splits(places)
    rows = [ch, ch, cm, cm, ch, cl]

    pl.semaphore_wait(barrier, group - 1)

    copies = []
    for shift in range(1, n_elem):
        other = lax.rem(my_elem + shift, n_elem)
        copy = pltpu.make_async_remote_copy(
            src_ref=panel_slots.at[my_elem],
            dst_ref=panel_slots.at[my_elem],
            send_sem=panel_send.at[shift],
            recv_sem=panel_recv.at[shift],
            device_id={"elem": other},
            device_id_type=MESH,
        )
        copy.start()
        copies.append(copy)

    fields = surface_ref[...].astype(jnp.float32).T
    for copy in copies:
        copy.wait()

    patch = patch_ref[...]
    slot = lax.broadcasted_iota(jnp.int32, (128, elements), 0)
    facets = jnp.zeros((8, elements), jnp.float32)
    for index in range(n_elem):
        hit = (slot + index * panel_count == patch) & (slot < panel_count)
        facets = facets + jnp.dot(
            panel_slots[index], hit.astype(jnp.float32),
            precision=lax.Precision.HIGHEST, preferred_element_type=jnp.float32,
        )

    stacked = jnp.concatenate(
        rows
        + [jnp.zeros((SPLIT_ROWS - 18, elements), jnp.float32), facets]
        + [jnp.zeros((128 - SPLIT_ROWS - 8, elements), jnp.float32)],
        axis=0,
    ).T
    place_split[...] = stacked[:, 0:SPLIT_ROWS].astype(jnp.bfloat16)
    area_cols[...] = jnp.broadcast_to(stacked[:, SPLIT_ROWS + 3:SPLIT_ROWS + 4], (elements, 128))

    for part in range(4):
        if part < 3:
            real = fields[0:cases] * facets[part:part + 1]
            imag = fields[cases:half] * facets[part:part + 1]
        else:
            real = fields[half:half + cases]
            imag = fields[half + cases:]
        first = part * half
        weights[first:first + cases, 0:elements] = imag.astype(jnp.bfloat16)
        weights[first + cases:first + half, 0:elements] = (-real).astype(jnp.bfloat16)
        weights[first:first + cases, elements:] = (-real).astype(jnp.bfloat16)
        weights[first + cases:first + half, elements:] = (-imag).astype(jnp.bfloat16)

    def block_sums(block):
        columns = pl.ds(pl.multiple_of(block * width, width), width)
        units = unit_split[:, columns]
        sums = jnp.zeros((4 * half, width), jnp.float32)
        for first in range(0, elements, TILE):
            tile = slice(first, first + TILE)
            turns = jnp.dot(place_split[tile], units, preferred_element_type=jnp.float32)
            turns = turns - jnp.round(turns)
            square = turns * turns
            area = jnp.concatenate([area_cols[tile]] * (width // 128), axis=1)
            cosine = (area * horner(COS_TURN, square)).astype(jnp.bfloat16)
            sine = (area * (turns * horner(SIN_TURN, square))).astype(jnp.bfloat16)
            sums = sums + jnp.dot(weights[:, tile], cosine, preferred_element_type=jnp.float32)
            sums = sums + jnp.dot(
                weights[:, elements + first:elements + first + TILE], sine,
                preferred_element_type=jnp.float32,
            )
        value = sums[3 * half:]
        for part in range(3):
            value = value + sums[part * half:(part + 1) * half] * unit_rows[part:part + 1, columns]
        return value

    def block_copy(step):
        away_elem = n_elem - 1 - lax.rem(step, n_elem)
        away_dir = n_dir - 1 - step // n_elem
        to_elem = lax.rem(my_elem + away_elem, n_elem)
        to_dir = lax.rem(my_dir + away_dir, n_dir)
        copy = pltpu.make_async_remote_copy(
            src_ref=outbox.at[step],
            dst_ref=inbox.at[step],
            send_sem=send_sem.at[step],
            recv_sem=recv_sem.at[step],
            device_id={"elem": to_elem, "dir": to_dir},
            device_id_type=MESH,
        )
        return copy, to_elem * n_dir + to_dir

    def send_block(step, carry):
        copy, block = block_copy(step)
        outbox[step] = block_sums(block).astype(jnp.bfloat16)
        copy.start()
        return carry

    lax.fori_loop(0, group - 1, send_block, 0)
    total[...] = block_sums(me)

    def take_block(step, carry):
        copy, _ = block_copy(step)
        copy.wait()
        total[...] += inbox[step].astype(jnp.float32)
        return carry

    lax.fori_loop(0, group - 1, take_block, 0)
    scale = wave * (1.0 / (4.0 * math.pi * math.sqrt(elements * group)))
    out_ref[...] = total[...] * scale


def fused(n_elem, n_dir, surface, centres, patch_of, panels, dir_index, wavenumber):
    elements, channels = surface.shape
    directions = dir_index.shape[0]
    group = n_elem * n_dir
    width = directions // group
    half = channels // 2
    vmem = pl.BlockSpec(memory_space=pltpu.VMEM)
    result = pl.pallas_call(
        functools.partial(kernel, n_elem, n_dir),
        out_shape=jax.ShapeDtypeStruct((half, width), jnp.float32),
        in_specs=[pl.BlockSpec(memory_space=pltpu.SMEM)] + [vmem] * 5,
        out_specs=vmem,
        scratch_shapes=[
            pltpu.VMEM((n_elem, 8, 128), jnp.float32),
            pltpu.VMEM((8, directions), jnp.float32),
            pltpu.VMEM((SPLIT_ROWS, directions), jnp.bfloat16),
            pltpu.VMEM((elements, SPLIT_ROWS), jnp.bfloat16),
            pltpu.VMEM((elements, 128), jnp.float32),
            pltpu.VMEM((4 * half, 2 * elements), jnp.bfloat16),
            pltpu.VMEM((group - 1, half, width), jnp.bfloat16),
            pltpu.VMEM((group - 1, half, width), jnp.bfloat16),
            pltpu.VMEM((half, width), jnp.float32),
            pltpu.SemaphoreType.DMA((n_elem,)),
            pltpu.SemaphoreType.DMA((n_elem,)),
            pltpu.SemaphoreType.DMA((group - 1,)),
            pltpu.SemaphoreType.DMA((group - 1,)),
        ],
        compiler_params=pltpu.CompilerParams(
            collective_id=0, has_side_effects=True, vmem_limit_bytes=40 * 1024 * 1024
        ),
        name="far_field",
    )(
        wavenumber, surface, centres, patch_of.reshape(1, elements), panels,
        dir_index.reshape(1, directions),
    )
    return result.reshape(2, half // 2, width)


def unit_vectors(dir_index):
    polar_angle = (dir_index // GRID_PHI).astype(jnp.float32) * (math.pi / (GRID_THETA - 1))
    azimuth = (dir_index % GRID_PHI).astype(jnp.float32) * (2.0 * math.pi / GRID_PHI)
    return jnp.stack(
        [
            jnp.sin(polar_angle) * jnp.cos(azimuth),
            jnp.sin(polar_angle) * jnp.sin(azimuth),
            jnp.cos(polar_angle),
        ]
    )


def far_block(fields, places, facets, unit_dirs, wave_number):
    phase_angle = wave_number * sum(places[d][:, None] * unit_dirs[d][None, :] for d in range(3))
    facing = sum(facets[d][:, None] * unit_dirs[d][None, :] for d in range(3))
    mono_real = facets[3][:, None] * jnp.cos(phase_angle)
    mono_imag = -facets[3][:, None] * jnp.sin(phase_angle)
    dipole = jnp.concatenate([mono_real * facing, mono_imag * facing], axis=1)
    monopole = jnp.concatenate([mono_real, mono_imag], axis=1)
    half = fields.shape[1] // 2
    cases, width = half // 2, unit_dirs.shape[1]
    sums = sum(
        lax.dot_general(
            part, source.astype(jnp.bfloat16), (((0,), (0,)), ((), ())),
            preferred_element_type=jnp.float32,
        )
        for part, source in ((fields[:, :half], dipole), (fields[:, half:], monopole))
    )
    sum_real = sums[:cases, :width] - sums[cases:, width:]
    sum_imag = sums[cases:, :width] + sums[:cases, width:]
    return jnp.stack([sum_imag, -sum_real])


def scattered(n_elem, n_dir, surface, centres, patch_of, panels, dir_index, wavenumber):
    panel_rows = lax.all_gather(panels, "elem", axis=1, tiled=True)
    facets = panel_rows[:, patch_of]
    unit_dirs = unit_vectors(dir_index)
    directions = dir_index.shape[0]
    width = math.gcd(512, directions)
    blocks = unit_dirs.reshape(3, -1, width).transpose(1, 0, 2)
    partials = lax.map(
        lambda block: far_block(surface, centres, facets, block, wavenumber[0]), blocks
    )
    partials = partials.transpose(1, 2, 0, 3).reshape(2, partials.shape[2], directions)
    summed = lax.psum_scatter(partials, ("elem", "dir"), scatter_dimension=2, tiled=True)
    elements = surface.shape[0] * n_elem * n_dir
    return summed * (wavenumber[0] / (4.0 * math.pi * math.sqrt(elements)))


def solution(mesh):
    n_elem, n_dir = mesh.shape["elem"], mesh.shape["dir"]

    def on_device(surface, centres, patch_of, panels, dir_index, wavenumber):
        width = dir_index.shape[0] // (n_elem * n_dir)
        aligned = width % 128 == 0 and surface.shape[0] % TILE == 0 and panels.shape[1] <= 128
        form = fused if aligned else scattered
        return form(n_elem, n_dir, surface, centres, patch_of, panels, dir_index, wavenumber)

    placed = (
        P(("parts", "elem", "dir"), None),
        P(None, ("elem", "dir")),
        P(("elem", "dir")),
        P(None, "elem"),
        P(),
        P("parts"),
    )
    return jax.shard_map(
        on_device,
        mesh=mesh,
        in_specs=placed,
        out_specs=P("parts", None, ("elem", "dir")),
        check_vma=False,
    )
```

```python
import functools
import math

import jax
import jax.numpy as jnp
import numpy as np
from jax import lax
from jax.experimental import pallas as pl
from jax.experimental.pallas import tpu as pltpu
from jax.sharding import PartitionSpec as P

GRID_THETA = 91
GRID_PHI = 180
QUARTER = GRID_PHI // 4
SPLIT_ROWS = 32
TILE = 256
VMEM_BYTES = 60 * 1024 * 1024
MESH = pl.DeviceIdType.MESH


def fit_even(function, degree, top):
    nodes = np.cos((np.arange(400) + 0.5) * np.pi / 800)
    scaled = nodes * top
    basis = np.stack([scaled ** (2 * power) for power in range(degree + 1)], axis=1)
    weights, *_ = np.linalg.lstsq(basis / 1.0, function(scaled), rcond=None)
    return [float(weight) for weight in weights]


SIN_HALF = fit_even(lambda r: np.sin(np.pi * r) / r, 3, 0.5)
COS_HALF = fit_even(lambda r: np.cos(np.pi * r), 3, 0.5)
SIN_QUARTER = fit_even(lambda r: np.sin(2 * np.pi * r) / r, 6, 0.25)


def horner(weights, z):
    value = jnp.float32(weights[-1])
    for weight in weights[-2::-1]:
        value = value * z + jnp.float32(weight)
    return value


def monic(weights):
    w0, w1, w2, w3 = weights
    b, c = w2 / w3, w1 / w3
    return w3, b, c, w0 / w3 - b * c


SIN_SCALE, *SIN_TERMS = monic(SIN_HALF)
COS_SCALE, *COS_TERMS = monic(COS_HALF)


def cubic(terms, z, z_squared):
    b, c, d = terms
    return (z + b) * (z_squared + c) + d


def splits(value):
    high = value.astype(jnp.bfloat16).astype(jnp.float32)
    rest = value - high
    middle = rest.astype(jnp.bfloat16).astype(jnp.float32)
    low = (rest - middle).astype(jnp.bfloat16).astype(jnp.float32)
    return high, middle, low


def grid_directions(dir_row):
    polar = jnp.floor((dir_row.astype(jnp.float32) + 0.5) * (1.0 / GRID_PHI))
    azimuth = dir_row.astype(jnp.float32) - polar * GRID_PHI
    row = lax.broadcasted_iota(jnp.int32, (8, dir_row.shape[1]), 0)
    steps = jnp.where(row < 2, polar, azimuth)
    steps = steps + jnp.where(row % 2 == 1, float(QUARTER), 0.0)
    steps = jnp.where(steps >= 2.0 * QUARTER, steps - 4.0 * QUARTER, steps)
    steps = jnp.where(steps > QUARTER, 2.0 * QUARTER - steps, steps)
    steps = jnp.where(steps < -QUARTER, -2.0 * QUARTER - steps, steps)
    turns = steps * (1.0 / GRID_PHI)
    sines = turns * horner(SIN_QUARTER, turns * turns)
    return sines[0:1] * sines[3:4], sines[0:1] * sines[2:3], sines[1:2]


def kernel(
    n_elem, n_dir,
    wave_ref, surface_hbm, centres_hbm, patch_hbm, panels_hbm, dir_hbm, out_ref,
    surface_ref, centres_ref, patch_ref, panels_ref, dir_ref, load_sem,
    panel_slots, unit_rows, unit_split, place_split, area_cols, weights, outbox, inbox, mono_even, mono_odd, field_rows, early,
    panel_send, panel_recv, send_sem, recv_sem,
):
    my_elem, my_dir = lax.axis_index("elem"), lax.axis_index("dir")
    me = my_elem * n_dir + my_dir
    group = n_elem * n_dir
    elements = surface_hbm.shape[0]
    width = out_ref.shape[1]
    half = surface_hbm.shape[1] // 2
    cases = half // 2
    panel_count = panels_hbm.shape[1]

    barrier = pltpu.get_barrier_semaphore()

    loads = [
        pltpu.make_async_copy(source, target, load_sem.at[index])
        for index, (source, target) in enumerate(
            [
                (panels_hbm, panels_ref),
                (dir_hbm, dir_ref),
                (centres_hbm, centres_ref),
                (patch_hbm, patch_ref),
                (surface_hbm, surface_ref),
            ]
        )
    ]
    for load in loads:
        load.start()

    def greet(step, carry):
        other = lax.rem(me + step, group)
        pl.semaphore_signal(
            barrier, inc=1,
            device_id={"elem": other // n_dir, "dir": lax.rem(other, n_dir)},
            device_id_type=MESH,
        )
        return carry

    lax.fori_loop(1, group, greet, 0)

    loads[0].wait()
    panel_slots[my_elem] = jnp.zeros((8, 128), jnp.float32)
    panel_slots[my_elem, 0:4, 0:panel_count] = panels_ref[...]

    loads[1].wait()
    ux, uy, uz = grid_directions(dir_ref[...])
    unit_rows[0:1, :] = ux
    unit_rows[1:2, :] = uy
    unit_rows[2:3, :] = uz
    uh, um, ul = zip(*[splits(u) for u in (ux, uy, uz)])
    pad = jnp.zeros((SPLIT_ROWS - 18, ux.shape[1]), jnp.float32)
    unit_split[...] = jnp.concatenate(
        [*uh, *um, *uh, *um, *ul, *uh, pad], axis=0
    ).astype(jnp.bfloat16)

    loads[2].wait()
    wave = wave_ref[0]
    places = centres_ref[...] * (wave * (0.5 / math.pi))
    ch, cm, cl = splits(places)

    pl.semaphore_wait(barrier, group - 1)

    copies = []
    for shift in range(1, n_elem):
        other = lax.rem(my_elem + shift, n_elem)
        copy = pltpu.make_async_remote_copy(
            src_ref=panel_slots.at[my_elem],
            dst_ref=panel_slots.at[my_elem],
            send_sem=panel_send.at[shift],
            recv_sem=panel_recv.at[shift],
            device_id={"elem": other},
            device_id_type=MESH,
        )
        copy.start()
        copies.append(copy)

    stacked = jnp.concatenate(
        [ch, ch, cm, cm, ch, cl, jnp.zeros((128 - 18, elements), jnp.float32)], axis=0
    ).T
    place_split[...] = stacked[:, 0:SPLIT_ROWS].astype(jnp.bfloat16)
    loads[3].wait()
    loads[4].wait()
    fields = surface_ref[...].astype(jnp.float32).T
    field_rows[...] = fields

    def receiver(step):
        away_elem = n_elem - 1 - step % n_elem
        away_dir = n_dir - 1 - step // n_elem
        return lax.rem(my_elem + away_elem, n_elem), lax.rem(my_dir + away_dir, n_dir)

    def block_of(step):
        to_elem, to_dir = receiver(step)
        return to_elem * n_dir + to_dir

    def half_waves(block, tile):
        units = unit_split[:, pl.ds(pl.multiple_of(block * width, width), width)]
        turns = jnp.dot(place_split[tile], units, preferred_element_type=jnp.float32)
        turns = turns - jnp.round(turns)
        square = turns * turns
        fourth = square * square
        return turns * cubic(SIN_TERMS, square, fourth), cubic(COS_TERMS, square, fourth)

    for first in range(0, elements, TILE):
        half_sine, half_cosine = half_waves(block_of(0), slice(first, first + TILE))
        early[first:first + TILE] = half_sine
        early[elements + first:elements + first + TILE] = half_cosine

    for copy in copies:
        copy.wait()

    patch = patch_ref[...]
    slot = lax.broadcasted_iota(jnp.int32, (128, elements), 0)
    facets = jnp.zeros((8, elements), jnp.float32)
    for index in range(n_elem):
        hit = (slot + index * panel_count == patch) & (slot < panel_count)
        facets = facets + jnp.dot(
            panel_slots[index], hit.astype(jnp.float32),
            precision=lax.Precision.HIGHEST, preferred_element_type=jnp.float32,
        )

    stacked = jnp.concatenate([facets, jnp.zeros((128 - 8, elements), jnp.float32)], axis=0).T
    area_cols[...] = jnp.broadcast_to(stacked[:, 3:4], (elements, 128))
    fields = field_rows[...]

    for part in range(4):
        if part < 3:
            real = fields[0:cases] * facets[part:part + 1]
            imag = fields[cases:half] * facets[part:part + 1]
        else:
            real = fields[half:half + cases]
            imag = fields[half + cases:]
        first = part * half
        real, imag = (-real).astype(jnp.bfloat16), imag.astype(jnp.bfloat16)
        for start in range(0, elements, TILE):
            tile = slice(start, start + TILE)
            cosine, sine = (slice(2 * start + s, 2 * start + s + TILE) for s in (0, TILE))
            weights[first:first + cases, cosine] = imag[:, tile]
            weights[first + cases:first + half, cosine] = real[:, tile]
            weights[first:first + cases, sine] = real[:, tile]
            weights[first + cases:first + half, sine] = -imag[:, tile]

    def block_columns(block):
        return pl.ds(pl.multiple_of(block * width, width), width)

    def fold(sums, block):
        value = sums[3 * half:]
        for part in range(3):
            value = value + (
                sums[part * half:(part + 1) * half] * unit_rows[part:part + 1, block_columns(block)]
            )
        return value

    def tile_sums(first, mono):
        tile = slice(2 * first, 2 * first + 2 * TILE)
        return jnp.dot(weights[:, tile], mono[tile], preferred_element_type=jnp.float32)

    def tile_waves(block, first, mono):
        tile = slice(first, first + TILE)
        if block is None:
            half_sine, half_cosine = early[tile], early[elements + first:elements + first + TILE]
        else:
            half_sine, half_cosine = half_waves(block, tile)
        area = area_cols[tile]
        area_cosine = area * (2.0 * SIN_SCALE * SIN_SCALE)
        area_sine = area * (2.0 * SIN_SCALE * COS_SCALE)
        for lane in range(0, width, 128):
            lanes = slice(lane, lane + 128)
            s, c = half_sine[:, lanes], half_cosine[:, lanes]
            mono[2 * first:2 * first + TILE, lanes] = (
                area - area_cosine * (s * s)
            ).astype(jnp.bfloat16)
            mono[2 * first + TILE:2 * first + 2 * TILE, lanes] = (
                area_sine * (s * c)
            ).astype(jnp.bfloat16)

    def block_copy(step):
        to_elem, to_dir = receiver(step)
        copy = pltpu.make_async_remote_copy(
            src_ref=outbox.at[step],
            dst_ref=inbox.at[step],
            send_sem=send_sem.at[step],
            recv_sem=recv_sem.at[step],
            device_id={"elem": to_elem, "dir": to_dir},
            device_id_type=MESH,
        )
        return copy, to_elem * n_dir + to_dir

    def block_sums(block, mono, next_block, next_mono):
        sums = None
        for first in range(0, elements, TILE):
            part = tile_sums(first, mono)
            sums = part if sums is None else sums + part
            if next_mono is not None:
                tile_waves(next_block, first, next_mono)
        return fold(sums, block)

    def send_block(step, mono, next_mono):
        copy, block = block_copy(step)
        value = block_sums(block, mono, block_of(step + 1), next_mono)
        outbox[step] = value.astype(jnp.bfloat16)
        copy.start()

    def send_pair(pair, carry):
        send_block(2 * pair, mono_even, mono_odd)
        send_block(2 * pair + 1, mono_odd, mono_even)
        return carry

    for first in range(0, elements, TILE):
        tile_waves(None, first, mono_even)
    lax.fori_loop(0, (group - 2) // 2, send_pair, 0)
    send_block(group - 2, mono_even, mono_odd)
    result = block_sums(me, mono_odd, None, None)
    for step in range(group - 1):
        block_copy(step)[0].wait()
        result = result + inbox[step].astype(jnp.float32)
    scale = wave * (1.0 / (4.0 * math.pi * math.sqrt(elements * group)))
    out_ref[...] = result * scale


def fused(n_elem, n_dir, surface, centres, patch_of, panels, dir_index, wavenumber):
    elements, channels = surface.shape
    directions = dir_index.shape[0]
    group = n_elem * n_dir
    width = directions // group
    half = channels // 2
    vmem = pl.BlockSpec(memory_space=pltpu.VMEM)
    result = pl.pallas_call(
        functools.partial(kernel, n_elem, n_dir),
        out_shape=jax.ShapeDtypeStruct((half, width), jnp.float32),
        in_specs=[pl.BlockSpec(memory_space=pltpu.SMEM)] + [pl.BlockSpec(memory_space=pltpu.HBM)] * 5,
        out_specs=vmem,
        scratch_shapes=[
            pltpu.VMEM((elements, channels), surface.dtype),
            pltpu.VMEM((3, elements), jnp.float32),
            pltpu.VMEM((1, elements), jnp.int32),
            pltpu.VMEM(panels.shape, jnp.float32),
            pltpu.VMEM((1, directions), jnp.int32),
            pltpu.SemaphoreType.DMA((5,)),
            pltpu.VMEM((n_elem, 8, 128), jnp.float32),
            pltpu.VMEM((8, directions), jnp.float32),
            pltpu.VMEM((SPLIT_ROWS, directions), jnp.bfloat16),
            pltpu.VMEM((elements, SPLIT_ROWS), jnp.bfloat16),
            pltpu.VMEM((elements, 128), jnp.float32),
            pltpu.VMEM((4 * half, 2 * elements), jnp.bfloat16),
            pltpu.VMEM((group - 1, half, width), jnp.bfloat16),
            pltpu.VMEM((group - 1, half, width), jnp.bfloat16),
            pltpu.VMEM((2 * elements, width), jnp.bfloat16),
            pltpu.VMEM((2 * elements, width), jnp.bfloat16),
            pltpu.VMEM((channels, elements), jnp.float32),
            pltpu.VMEM((2 * elements, width), jnp.float32),
            pltpu.SemaphoreType.DMA((n_elem,)),
            pltpu.SemaphoreType.DMA((n_elem,)),
            pltpu.SemaphoreType.DMA((group - 1,)),
            pltpu.SemaphoreType.DMA((group - 1,)),
        ],
        compiler_params=pltpu.CompilerParams(
            collective_id=0, has_side_effects=True, vmem_limit_bytes=VMEM_BYTES
        ),
        name="far_field",
    )(
        wavenumber, surface, centres, patch_of.reshape(1, elements), panels,
        dir_index.reshape(1, directions),
    )
    return result.reshape(2, half // 2, width)


def unit_vectors(dir_index):
    polar_angle = (dir_index // GRID_PHI).astype(jnp.float32) * (math.pi / (GRID_THETA - 1))
    azimuth = (dir_index % GRID_PHI).astype(jnp.float32) * (2.0 * math.pi / GRID_PHI)
    return jnp.stack(
        [
            jnp.sin(polar_angle) * jnp.cos(azimuth),
            jnp.sin(polar_angle) * jnp.sin(azimuth),
            jnp.cos(polar_angle),
        ]
    )


def far_block(fields, places, facets, unit_dirs, wave_number):
    phase_angle = wave_number * sum(places[d][:, None] * unit_dirs[d][None, :] for d in range(3))
    facing = sum(facets[d][:, None] * unit_dirs[d][None, :] for d in range(3))
    mono_real = facets[3][:, None] * jnp.cos(phase_angle)
    mono_imag = -facets[3][:, None] * jnp.sin(phase_angle)
    dipole = jnp.concatenate([mono_real * facing, mono_imag * facing], axis=1)
    monopole = jnp.concatenate([mono_real, mono_imag], axis=1)
    half = fields.shape[1] // 2
    cases, width = half // 2, unit_dirs.shape[1]
    sums = sum(
        lax.dot_general(
            part, source.astype(jnp.bfloat16), (((0,), (0,)), ((), ())),
            preferred_element_type=jnp.float32,
        )
        for part, source in ((fields[:, :half], dipole), (fields[:, half:], monopole))
    )
    sum_real = sums[:cases, :width] - sums[cases:, width:]
    sum_imag = sums[cases:, :width] + sums[:cases, width:]
    return jnp.stack([sum_imag, -sum_real])


def scattered(n_elem, n_dir, surface, centres, patch_of, panels, dir_index, wavenumber):
    panel_rows = lax.all_gather(panels, "elem", axis=1, tiled=True)
    facets = panel_rows[:, patch_of]
    unit_dirs = unit_vectors(dir_index)
    directions = dir_index.shape[0]
    width = math.gcd(512, directions)
    blocks = unit_dirs.reshape(3, -1, width).transpose(1, 0, 2)
    partials = lax.map(
        lambda block: far_block(surface, centres, facets, block, wavenumber[0]), blocks
    )
    partials = partials.transpose(1, 2, 0, 3).reshape(2, partials.shape[2], directions)
    summed = lax.psum_scatter(partials, ("elem", "dir"), scatter_dimension=2, tiled=True)
    elements = surface.shape[0] * n_elem * n_dir
    return summed * (wavenumber[0] / (4.0 * math.pi * math.sqrt(elements)))


def solution(mesh):
    n_elem, n_dir = mesh.shape["elem"], mesh.shape["dir"]

    def on_device(surface, centres, patch_of, panels, dir_index, wavenumber):
        width = dir_index.shape[0] // (n_elem * n_dir)
        aligned = width % 128 == 0 and (n_elem * n_dir) % 2 == 0 and surface.shape[0] % TILE == 0 and panels.shape[1] <= 128
        form = fused if aligned else scattered
        return form(n_elem, n_dir, surface, centres, patch_of, panels, dir_index, wavenumber)

    placed = (
        P(("parts", "elem", "dir"), None),
        P(None, ("elem", "dir")),
        P(("elem", "dir")),
        P(None, "elem"),
        P(),
        P("parts"),
    )
    return jax.shard_map(
        on_device,
        mesh=mesh,
        in_specs=placed,
        out_specs=P("parts", None, ("elem", "dir")),
        check_vma=False,
    )
```

```python
import functools
import itertools
import math

import jax
import jax.numpy as jnp
import numpy as np
from jax import lax
from jax.experimental import pallas as pl
from jax.experimental.pallas import tpu as pltpu
from jax.sharding import PartitionSpec as P

GRID_THETA = 91
GRID_PHI = 180
QUARTER = GRID_PHI // 4
SPLIT_ROWS = 32
TILE = 256
VMEM_BYTES = 60 * 1024 * 1024
MESH = pl.DeviceIdType.MESH


def fit_even(function, degree, top):
    nodes = np.cos((np.arange(400) + 0.5) * np.pi / 800)
    scaled = nodes * top
    basis = np.stack([scaled ** (2 * power) for power in range(degree + 1)], axis=1)
    weights, *_ = np.linalg.lstsq(basis / 1.0, function(scaled), rcond=None)
    return [float(weight) for weight in weights]


SIN_HALF = fit_even(lambda r: np.sin(np.pi * r) / r, 3, 0.5)
COS_HALF = fit_even(lambda r: np.cos(np.pi * r), 3, 0.5)
SIN_QUARTER = fit_even(lambda r: np.sin(2 * np.pi * r) / r, 6, 0.25)


def horner(weights, z):
    value = jnp.float32(weights[-1])
    for weight in weights[-2::-1]:
        value = value * z + jnp.float32(weight)
    return value


def monic(weights):
    w0, w1, w2, w3 = weights
    b, c = w2 / w3, w1 / w3
    return w3, b, c, w0 / w3 - b * c


SIN_SCALE, *SIN_TERMS = monic(SIN_HALF)
COS_SCALE, *COS_TERMS = monic(COS_HALF)


def cubic(terms, z, z_squared):
    b, c, d = terms
    return (z + b) * (z_squared + c) + d


def splits(value):
    high = value.astype(jnp.bfloat16).astype(jnp.float32)
    rest = value - high
    middle = rest.astype(jnp.bfloat16).astype(jnp.float32)
    low = (rest - middle).astype(jnp.bfloat16).astype(jnp.float32)
    return high, middle, low


def grid_directions(dir_row):
    polar = jnp.floor((dir_row.astype(jnp.float32) + 0.5) * (1.0 / GRID_PHI))
    azimuth = dir_row.astype(jnp.float32) - polar * GRID_PHI
    row = lax.broadcasted_iota(jnp.int32, (8, dir_row.shape[1]), 0)
    steps = jnp.where(row < 2, polar, azimuth)
    steps = steps + jnp.where(row % 2 == 1, float(QUARTER), 0.0)
    steps = jnp.where(steps >= 2.0 * QUARTER, steps - 4.0 * QUARTER, steps)
    steps = jnp.where(steps > QUARTER, 2.0 * QUARTER - steps, steps)
    steps = jnp.where(steps < -QUARTER, -2.0 * QUARTER - steps, steps)
    turns = steps * (1.0 / GRID_PHI)
    sines = turns * horner(SIN_QUARTER, turns * turns)
    return sines[0:1] * sines[3:4], sines[0:1] * sines[2:3], sines[1:2]


def kernel(
    n_elem, n_dir,
    wave_ref, surface_hbm, centres_hbm, patch_hbm, panels_hbm, dir_hbm, out_ref,
    surface_ref, centres_ref, patch_ref, panels_ref, dir_ref, load_sem,
    panel_slots, unit_rows, unit_split, place_split, area_cols, weights, outbox, inbox, mono_even, mono_odd, field_rows, early,
    panel_send, panel_recv, pair_send, pair_recv, send_sem, recv_sem,
):
    my_elem, my_dir = lax.axis_index("elem"), lax.axis_index("dir")
    me = my_elem * n_dir + my_dir
    pairs = n_elem // 2
    core, my_pair = lax.rem(my_elem, 2), my_elem // 2
    blocks = pairs * n_dir
    own = surface_hbm.shape[0]
    elements = 2 * own
    width = out_ref.shape[1]
    half = surface_hbm.shape[1] // 2
    cases = half // 2
    panel_count = panels_hbm.shape[1]

    barrier = pltpu.get_barrier_semaphore()

    loads = [
        pltpu.make_async_copy(source, target, load_sem.at[index])
        for index, (source, target) in enumerate(
            [
                (panels_hbm, panels_ref),
                (dir_hbm, dir_ref),
                (centres_hbm, centres_ref.at[0]),
                (patch_hbm, patch_ref.at[0]),
                (surface_hbm, surface_ref.at[0]),
            ]
        )
    ]
    for load in loads:
        load.start()

    def receiver(step):
        away_pair = pairs - 1 - step % pairs
        away_dir = n_dir - 1 - step // pairs
        to_elem = 2 * lax.rem(my_pair + away_pair, pairs) + core
        return to_elem, lax.rem(my_dir + away_dir, n_dir)

    def block_of(step):
        to_elem, to_dir = receiver(step)
        return to_elem * n_dir + to_dir

    def greet(elem, dir_):
        pl.semaphore_signal(
            barrier, inc=1, device_id={"elem": elem, "dir": dir_}, device_id_type=MESH
        )

    for index in range(pairs):
        greet(2 * lax.rem(my_pair + index, pairs) + 1 - core, my_dir)
    for step in range(blocks - 2, -1, -1):
        greet(*receiver(step))

    loads[0].wait()
    panel_slots[my_elem] = jnp.zeros((8, 128), jnp.float32)
    panel_slots[my_elem, 0:4, 0:panel_count] = panels_ref[...]

    loads[1].wait()
    ux, uy, uz = grid_directions(dir_ref[...])
    unit_rows[0:1, :] = ux
    unit_rows[1:2, :] = uy
    unit_rows[2:3, :] = uz
    uh, um, ul = zip(*[splits(u) for u in (ux, uy, uz)])
    pad = jnp.zeros((SPLIT_ROWS - 18, ux.shape[1]), jnp.float32)
    unit_split[...] = jnp.concatenate(
        [*uh, *um, *uh, *um, *ul, *uh, pad], axis=0
    ).astype(jnp.bfloat16)

    wave = wave_ref[0]

    def load_half(side):
        rows = slice(side * own, (side + 1) * own)
        places = centres_ref[side] * (wave * (0.5 / math.pi))
        ch, cm, cl = splits(places)
        stacked = jnp.concatenate(
            [ch, ch, cm, cm, ch, cl, jnp.zeros((128 - 18, own), jnp.float32)], axis=0
        ).T
        place_split[rows] = stacked[:, 0:SPLIT_ROWS].astype(jnp.bfloat16)
        field_rows[:, rows] = surface_ref[side].astype(jnp.float32).T

    pl.semaphore_wait(barrier, blocks - 1 + pairs)

    copies = []
    for shift in range(1, n_elem):
        other = lax.rem(my_elem + shift, n_elem)
        copy = pltpu.make_async_remote_copy(
            src_ref=panel_slots.at[my_elem],
            dst_ref=panel_slots.at[my_elem],
            send_sem=panel_send.at[shift],
            recv_sem=panel_recv.at[shift],
            device_id={"elem": other},
            device_id_type=MESH,
        )
        copy.start()
        copies.append(copy)

    for index, (source, target) in enumerate(
        [(centres_hbm, centres_ref), (patch_hbm, patch_ref), (surface_hbm, surface_ref)]
    ):
        copy = pltpu.make_async_remote_copy(
            src_ref=source,
            dst_ref=target.at[1],
            send_sem=pair_send.at[index],
            recv_sem=pair_recv.at[index],
            device_id={"elem": my_elem + 1 - 2 * core},
            device_id_type=MESH,
        )
        copy.start()
        copies.append(copy)

    for load in loads[2:]:
        load.wait()
    load_half(0)

    def half_waves(block, tile):
        units = unit_split[:, pl.ds(pl.multiple_of(block * width, width), width)]
        turns = jnp.dot(place_split[tile], units, preferred_element_type=jnp.float32)
        turns = turns - jnp.round(turns)
        square = turns * turns
        fourth = square * square
        return turns * cubic(SIN_TERMS, square, fourth), cubic(COS_TERMS, square, fourth)

    for index in range(2):
        for first in range(0, own, TILE):
            half_sine, half_cosine = half_waves(block_of(index), slice(first, first + TILE))
            early[index, first:first + TILE] = half_sine
            early[index, own + first:own + first + TILE] = half_cosine

    for copy in copies:
        copy.wait()

    load_half(1)

    patch = jnp.concatenate([patch_ref[0], patch_ref[1]], axis=1)
    slot = lax.broadcasted_iota(jnp.int32, (128, elements), 0)
    facets = jnp.zeros((8, elements), jnp.float32)
    for index in range(n_elem):
        hit = (slot + index * panel_count == patch) & (slot < panel_count)
        facets = facets + jnp.dot(
            panel_slots[index], hit.astype(jnp.float32),
            precision=lax.Precision.HIGHEST, preferred_element_type=jnp.float32,
        )

    stacked = jnp.concatenate([facets, jnp.zeros((128 - 8, elements), jnp.float32)], axis=0).T
    area_cols[...] = jnp.broadcast_to(stacked[:, 3:4], (elements, 128))
    fields = field_rows[...]

    for part in range(4):
        if part < 3:
            real = fields[0:cases] * facets[part:part + 1]
            imag = fields[cases:half] * facets[part:part + 1]
        else:
            real = fields[half:half + cases]
            imag = fields[half + cases:]
        first = part * half
        real, imag = (-real).astype(jnp.bfloat16), imag.astype(jnp.bfloat16)
        for start in range(0, elements, TILE):
            tile = slice(start, start + TILE)
            cosine, sine = (slice(2 * start + s, 2 * start + s + TILE) for s in (0, TILE))
            weights[first:first + cases, cosine] = imag[:, tile]
            weights[first + cases:first + half, cosine] = real[:, tile]
            weights[first:first + cases, sine] = real[:, tile]
            weights[first + cases:first + half, sine] = -imag[:, tile]

    def block_columns(block):
        return pl.ds(pl.multiple_of(block * width, width), width)

    def fold(sums, block):
        value = sums[3 * half:]
        for part in range(3):
            value = value + (
                sums[part * half:(part + 1) * half] * unit_rows[part:part + 1, block_columns(block)]
            )
        return value

    def tile_sums(first, mono):
        tile = slice(2 * first, 2 * first + 2 * TILE)
        return jnp.dot(weights[:, tile], mono[tile], preferred_element_type=jnp.float32)

    def tile_waves(block, first, mono, stash=None):
        tile = slice(first, first + TILE)
        if stash is not None and first < own:
            half_sine, half_cosine = early[stash, tile], early[stash, own + first:own + first + TILE]
        else:
            half_sine, half_cosine = half_waves(block, tile)
        area = area_cols[tile]
        area_cosine = area * (2.0 * SIN_SCALE * SIN_SCALE)
        area_sine = area * (2.0 * SIN_SCALE * COS_SCALE)
        for lane in range(0, width, 128):
            lanes = slice(lane, lane + 128)
            s, c = half_sine[:, lanes], half_cosine[:, lanes]
            mono[2 * first:2 * first + TILE, lanes] = (
                area - area_cosine * (s * s)
            ).astype(jnp.bfloat16)
            mono[2 * first + TILE:2 * first + 2 * TILE, lanes] = (
                area_sine * (s * c)
            ).astype(jnp.bfloat16)

    def block_copy(step):
        to_elem, to_dir = receiver(step)
        copy = pltpu.make_async_remote_copy(
            src_ref=outbox.at[step],
            dst_ref=inbox.at[step],
            send_sem=send_sem.at[step],
            recv_sem=recv_sem.at[step],
            device_id={"elem": to_elem, "dir": to_dir},
            device_id_type=MESH,
        )
        return copy, to_elem * n_dir + to_dir

    tiles = list(range(0, elements, TILE))
    middle = len(tiles) // 2

    def block_sums(block, mono, next_block, next_mono, next_tiles, stash=None):
        sums = None
        for first, next_first in itertools.zip_longest(tiles, next_tiles):
            part = tile_sums(first, mono)
            sums = part if sums is None else sums + part
            if next_first is not None:
                tile_waves(next_block, next_first, next_mono, stash)
        return fold(sums, block)

    def send_block(step, mono, next_mono, next_tiles, stash=None):
        copy, block = block_copy(step)
        value = block_sums(block, mono, block_of(step + 1), next_mono, next_tiles, stash)
        outbox[step] = value.astype(jnp.bfloat16)
        copy.start()

    def send_pair(pair, carry):
        send_block(2 * pair, mono_even, mono_odd, tiles)
        send_block(2 * pair + 1, mono_odd, mono_even, tiles)
        return carry

    for first in tiles:
        tile_waves(block_of(0), first, mono_even, 0)
    send_block(0, mono_even, mono_odd, tiles, 1)
    send_block(1, mono_odd, mono_even, tiles)
    lax.fori_loop(1, (blocks - 2) // 2, send_pair, 0)
    send_block(blocks - 2, mono_even, mono_odd, tiles[:middle])
    result = block_sums(me, mono_odd, me, mono_odd, tiles[middle:])
    for step in range(blocks - 1):
        block_copy(step)[0].wait()
        result = result + inbox[step].astype(jnp.float32)
    scale = wave * (1.0 / (4.0 * math.pi * math.sqrt(own * n_elem * n_dir)))
    out_ref[...] = result * scale


def fused(n_elem, n_dir, surface, centres, patch_of, panels, dir_index, wavenumber):
    own, channels = surface.shape
    elements = 2 * own
    directions = dir_index.shape[0]
    blocks = n_elem // 2 * n_dir
    width = directions // (n_elem * n_dir)
    half = channels // 2
    vmem = pl.BlockSpec(memory_space=pltpu.VMEM)
    result = pl.pallas_call(
        functools.partial(kernel, n_elem, n_dir),
        out_shape=jax.ShapeDtypeStruct((half, width), jnp.float32),
        in_specs=[pl.BlockSpec(memory_space=pltpu.SMEM)] + [pl.BlockSpec(memory_space=pltpu.HBM)] * 5,
        out_specs=vmem,
        scratch_shapes=[
            pltpu.VMEM((2, own, channels), surface.dtype),
            pltpu.VMEM((2, 3, own), jnp.float32),
            pltpu.VMEM((2, 1, own), jnp.int32),
            pltpu.VMEM(panels.shape, jnp.float32),
            pltpu.VMEM((1, directions), jnp.int32),
            pltpu.SemaphoreType.DMA((5,)),
            pltpu.VMEM((n_elem, 8, 128), jnp.float32),
            pltpu.VMEM((8, directions), jnp.float32),
            pltpu.VMEM((SPLIT_ROWS, directions), jnp.bfloat16),
            pltpu.VMEM((elements, SPLIT_ROWS), jnp.bfloat16),
            pltpu.VMEM((elements, 128), jnp.float32),
            pltpu.VMEM((4 * half, 2 * elements), jnp.bfloat16),
            pltpu.VMEM((blocks - 1, half, width), jnp.bfloat16),
            pltpu.VMEM((blocks - 1, half, width), jnp.bfloat16),
            pltpu.VMEM((2 * elements, width), jnp.bfloat16),
            pltpu.VMEM((2 * elements, width), jnp.bfloat16),
            pltpu.VMEM((channels, elements), jnp.float32),
            pltpu.VMEM((2, 2 * own, width), jnp.float32),
            pltpu.SemaphoreType.DMA((n_elem,)),
            pltpu.SemaphoreType.DMA((n_elem,)),
            pltpu.SemaphoreType.DMA((3,)),
            pltpu.SemaphoreType.DMA((3,)),
            pltpu.SemaphoreType.DMA((blocks - 1,)),
            pltpu.SemaphoreType.DMA((blocks - 1,)),
        ],
        compiler_params=pltpu.CompilerParams(
            collective_id=0, has_side_effects=True, vmem_limit_bytes=VMEM_BYTES
        ),
        name="far_field",
    )(
        wavenumber, surface, centres, patch_of.reshape(1, own), panels,
        dir_index.reshape(1, directions),
    )
    return result.reshape(2, half // 2, width)


def unit_vectors(dir_index):
    polar_angle = (dir_index // GRID_PHI).astype(jnp.float32) * (math.pi / (GRID_THETA - 1))
    azimuth = (dir_index % GRID_PHI).astype(jnp.float32) * (2.0 * math.pi / GRID_PHI)
    return jnp.stack(
        [
            jnp.sin(polar_angle) * jnp.cos(azimuth),
            jnp.sin(polar_angle) * jnp.sin(azimuth),
            jnp.cos(polar_angle),
        ]
    )


def far_block(fields, places, facets, unit_dirs, wave_number):
    phase_angle = wave_number * sum(places[d][:, None] * unit_dirs[d][None, :] for d in range(3))
    facing = sum(facets[d][:, None] * unit_dirs[d][None, :] for d in range(3))
    mono_real = facets[3][:, None] * jnp.cos(phase_angle)
    mono_imag = -facets[3][:, None] * jnp.sin(phase_angle)
    dipole = jnp.concatenate([mono_real * facing, mono_imag * facing], axis=1)
    monopole = jnp.concatenate([mono_real, mono_imag], axis=1)
    half = fields.shape[1] // 2
    cases, width = half // 2, unit_dirs.shape[1]
    sums = sum(
        lax.dot_general(
            part, source.astype(jnp.bfloat16), (((0,), (0,)), ((), ())),
            preferred_element_type=jnp.float32,
        )
        for part, source in ((fields[:, :half], dipole), (fields[:, half:], monopole))
    )
    sum_real = sums[:cases, :width] - sums[cases:, width:]
    sum_imag = sums[cases:, :width] + sums[:cases, width:]
    return jnp.stack([sum_imag, -sum_real])


def scattered(n_elem, n_dir, surface, centres, patch_of, panels, dir_index, wavenumber):
    panel_rows = lax.all_gather(panels, "elem", axis=1, tiled=True)
    facets = panel_rows[:, patch_of]
    unit_dirs = unit_vectors(dir_index)
    directions = dir_index.shape[0]
    width = math.gcd(512, directions)
    blocks = unit_dirs.reshape(3, -1, width).transpose(1, 0, 2)
    partials = lax.map(
        lambda block: far_block(surface, centres, facets, block, wavenumber[0]), blocks
    )
    partials = partials.transpose(1, 2, 0, 3).reshape(2, partials.shape[2], directions)
    summed = lax.psum_scatter(partials, ("elem", "dir"), scatter_dimension=2, tiled=True)
    elements = surface.shape[0] * n_elem * n_dir
    return summed * (wavenumber[0] / (4.0 * math.pi * math.sqrt(elements)))


def solution(mesh):
    n_elem, n_dir = mesh.shape["elem"], mesh.shape["dir"]

    def on_device(surface, centres, patch_of, panels, dir_index, wavenumber):
        width = dir_index.shape[0] // (n_elem * n_dir)
        aligned = width % 128 == 0 and n_elem % 2 == 0 and n_elem // 2 * n_dir % 2 == 0 and n_dir > 1 and surface.shape[0] % TILE == 0 and panels.shape[1] <= 128
        form = fused if aligned else scattered
        return form(n_elem, n_dir, surface, centres, patch_of, panels, dir_index, wavenumber)

    placed = (
        P(("parts", "elem", "dir"), None),
        P(None, ("elem", "dir")),
        P(("elem", "dir")),
        P(None, "elem"),
        P(),
        P("parts"),
    )
    return jax.shard_map(
        on_device,
        mesh=mesh,
        in_specs=placed,
        out_specs=P("parts", None, ("elem", "dir")),
        check_vma=False,
    )
```
